512 devices in a mesh: cp: 64 (over z, x), tp: 8 (over y, core).
Axes of the slice: x: 4, y: 4, z: 16, core: 2. Of those that a mesh axis runs over, the one named last changes fastest.
Arguments:
- queries: bfloat16 [32, 512, 8192], P(None, 'cp', 'tp'), may hold values from -6 to 6
- key_row_matrix: bfloat16 [32, 512, 1024], P(None, 'cp', 'tp'), may hold values from -6 to 6
- value_row_matrix: bfloat16 [32, 512, 1024], P(None, 'cp', 'tp'), may hold values from -6 to 6
- residual: bfloat16 [32, 512, 4096], P(None, 'cp', 'tp'), may hold values from -6 to 6
- out_weight: bfloat16 [64, 128, 4096], P('tp', 'cp'), may hold values from -0.09375 to 0.09375
- doc_bounds: int32 [129], replicated, may hold values from 0 to 16384, as said below
- owner_plan: int32 [128], replicated, may hold values from 0 to 63, as said below
Outputs:
- mixed: bfloat16 [32, 512, 4096], P(None, 'cp', 'tp')
- stats: float32 [64, 64, 512], P('cp', 'tp')
The draws below stay inside these ranges and needn't reach their ends.
Inputs may be any that keep to these rules, and one draw needn't show every extreme that they name: `doc_bounds`: increasing from 0 to 16384; every document length is a multiple of 8. `owner_plan`: each owner holds exactly two documents, and they are consecutive; the documents of one owner cover at most 64 blocks of 8 positions, and those of some owner exactly 64.
All inputs are finite; a program needn't handle non-finite values.
Results may differ from the reference program's by a relative error of at most 0.0034.
Values may be sent and summed in bfloat16 or wider, within the bound.
No kernel may reach another device: no remote copies, remote signals or barrier semaphores. Data moves between devices by JAX's collectives and lax.ppermute only.
A program may use at most 64 MiB of HBM per device.

```python
import math
import jax
import jax.numpy as jnp
from jax import lax

QUERY_HEADS = 64
KEY_VALUE_HEADS = 8
HEAD_SIZE = 128
DWIN = 4096
GROUP = 8
BLOCK_POSITIONS = 8
DEVICE_BLOCKS = 32
OWNER_ROW_SLOTS = 512
PACKED_TOKENS = 16384
N_CP = 64


def layout_plan(key):
    run_key, split_key, perm_key, full_key = jax.random.split(key, 4)
    full_run = jax.random.randint(full_key, (), 0, N_CP)
    chain_pos = jnp.arange(1, N_CP, dtype=jnp.int32)
    base_size = DEVICE_BLOCKS - (chain_pos <= DEVICE_BLOCKS).astype(jnp.int32)
    wiggle = jax.random.randint(run_key, (N_CP + 1,), 0, DEVICE_BLOCKS - 2)
    edge_ids = jnp.arange(N_CP + 1, dtype=jnp.int32)
    wiggle = jnp.where((edge_ids <= 1) | (edge_ids == N_CP), 0, wiggle)
    chain_sizes = base_size + wiggle[1:N_CP] - wiggle[2:N_CP + 1]
    run_sizes = jnp.zeros((N_CP,), jnp.int32).at[(full_run + chain_pos) % N_CP].set(chain_sizes)
    run_sizes = run_sizes.at[full_run].set(2 * DEVICE_BLOCKS)
    split_at = jax.random.randint(split_key, (N_CP,), 1, run_sizes)
    doc_blocks = jnp.stack([split_at, run_sizes - split_at], axis=1).reshape(-1)
    bounds = jnp.concatenate([jnp.zeros((1,), jnp.int32), jnp.cumsum(doc_blocks)]) * BLOCK_POSITIONS
    owners = jax.random.permutation(perm_key, N_CP)
    return (bounds.astype(jnp.int32), jnp.repeat(owners, 2).astype(jnp.int32))


def draw_doc_bounds(key, part):
    bounds, owners = layout_plan(key)
    return bounds


def draw_owner_plan(key, part):
    bounds, owners = layout_plan(key)
    return owners


def draw_queries(key, part):
    key = jax.random.fold_in(key, 11)
    drawn_value_rows = jnp.clip(jax.random.normal(key, (PACKED_TOKENS, QUERY_HEADS, HEAD_SIZE)), -4.0, 4.0)
    return drawn_value_rows.reshape(DEVICE_BLOCKS, N_CP * BLOCK_POSITIONS, QUERY_HEADS * HEAD_SIZE).astype(jnp.bfloat16)


def draw_key_row_matrix(key, part):
    key = jax.random.fold_in(key, 23)
    drawn_value_rows = jnp.clip(jax.random.normal(key, (PACKED_TOKENS, KEY_VALUE_HEADS, HEAD_SIZE)), -4.0, 4.0)
    return drawn_value_rows.reshape(DEVICE_BLOCKS, N_CP * BLOCK_POSITIONS, KEY_VALUE_HEADS * HEAD_SIZE).astype(jnp.bfloat16)


def strengthened(result, rng, source, target, shards_of, factor):
    owner, partner = [(jnp.arange(result.shape[dim]) // (result.shape[dim] // shards_of)).reshape([-1 if axis == dim else 1 for axis in range(result.ndim)]) for dim in (source, target)]
    chosen = jax.random.permutation(rng, shards_of)[partner]
    strong = (owner == chosen) | (owner == (partner + shards_of // 2) % shards_of)
    return jnp.where(strong, factor * result, result)


def shard_levels(stream_key, shape, cuts, least, top_value):
    factor_of, own = 1.0, jax.random.fold_in(stream_key, 6)
    for axis_at, parts in cuts:
        heights = jnp.exp(jax.random.uniform(jax.random.fold_in(own, axis_at), (parts,), jnp.float32, least / len(cuts), top_value / len(cuts)))
        factor_of = factor_of * jnp.repeat(heights, shape[axis_at] // parts).reshape([-1 if axis == axis_at else 1 for axis in range(len(shape))])
    return factor_of


def gaussian(key, extent, scale, reach, cuts=(), held_as=jnp.bfloat16):
    array = scale * jax.random.normal(key, extent, jnp.float32)
    if cuts:
        array = array * shard_levels(key, extent, cuts, -0.22, 0.18)
    return jnp.clip(array, -reach, reach).astype(held_as)


def gaussian_with(rng, shape, scale, most, pieces, heavy, kind=jnp.bfloat16):
    values = scale * jax.random.normal(rng, shape, jnp.float32)
    if pieces:
        values = values * shard_levels(rng, shape, pieces, -0.22, 0.18)
    return jnp.clip(strengthened(values, jax.random.fold_in(rng, 3), *heavy), -most, most).astype(kind)


def setup_inputs(seed: int = 0) -> dict:
    key_list = jax.random.split(jax.random.key(seed), 8)
    queries = draw_queries(jax.random.fold_in(key_list[7], 71), 0)
    key_row_matrix = draw_key_row_matrix(jax.random.fold_in(key_list[7], 71), 0)
    value_row_matrix = gaussian(key_list[2], (DEVICE_BLOCKS, OWNER_ROW_SLOTS, KEY_VALUE_HEADS * HEAD_SIZE), 1.0, 6.0, ((1, 64), (2, 8)))
    residual = gaussian(key_list[3], (DEVICE_BLOCKS, OWNER_ROW_SLOTS, DWIN), 1.0, 6.0, ((1, 64), (2, 8)))
    out_weight = gaussian_with(key_list[4], (QUERY_HEADS, HEAD_SIZE, DWIN), (QUERY_HEADS * HEAD_SIZE) ** -0.5, 0.09375, ((0, 8), (1, 64)), (0, 2, 8, 2.0))
    doc_bounds = draw_doc_bounds(jax.random.fold_in(key_list[7], 71), 0)
    owner_plan = draw_owner_plan(jax.random.fold_in(key_list[7], 71), 0)
    return dict(queries=queries, key_row_matrix=key_row_matrix, value_row_matrix=value_row_matrix, residual=residual, out_weight=out_weight, doc_bounds=doc_bounds, owner_plan=owner_plan)


MASKED = -1e+30

def doc_lookup(doc_bounds, positions):
    return lax.optimization_barrier(jnp.sum((doc_bounds[None, 1:] <= positions[:, None]).astype(jnp.int32), axis=1))

def owner_span(doc_bounds, owner_plan, owner, tokens, block_rows):
    mine = owner_plan == owner
    first_block = jnp.min(jnp.where(mine, doc_bounds[:-1], tokens)) // block_rows
    end_block = jnp.max(jnp.where(mine, doc_bounds[1:], 0)) // block_rows
    return (first_block.astype(jnp.int32), end_block.astype(jnp.int32))

def slot_positions(first_block, end_block, slot_count, block_rows):
    slot_ids = jnp.arange(slot_count, dtype=jnp.int32)
    block_ids = first_block + jnp.mod(slot_ids - first_block, slot_count)
    row_offsets = jnp.arange(block_rows, dtype=jnp.int32)
    positions = (block_ids[:, None] * block_rows + row_offsets[None, :]).reshape(-1)
    is_live = jnp.repeat(block_ids < end_block, block_rows)
    return (positions.astype(jnp.int32), is_live)

def attend_block(query_part, key_part, value_part, query_pos, query_doc, query_live, key_pos, key_doc, key_live, group):
    scale = 1.0 / math.sqrt(HEAD_SIZE)
    allowed = query_live[:, None] & key_live[None, :] & (query_doc[:, None] == key_doc[None, :]) & (key_pos[None, :] <= query_pos[:, None])
    allowed = allowed | (key_pos[None, :] == query_pos[:, None])
    head_ids = jnp.arange(query_part.shape[1], dtype=jnp.int32)

    def one_head(head):
        query_head = lax.dynamic_index_in_dim(query_part, head, 1, keepdims=False)
        key_head = lax.dynamic_index_in_dim(key_part, head // group, 1, keepdims=False)
        value_head = lax.dynamic_index_in_dim(value_part, head // group, 1, keepdims=False)
        scores = jnp.dot(query_head, key_head.T, preferred_element_type=jnp.float32) * scale
        scores = jnp.where(allowed, scores, MASKED)
        row_max = lax.optimization_barrier(jnp.max(scores, axis=1, keepdims=True))
        expo = jnp.where(allowed, jnp.exp(scores - row_max), 0.0)
        total = lax.optimization_barrier(jnp.sum(expo, axis=1, keepdims=True))
        weighted = jnp.dot(expo.astype(jnp.bfloat16), value_head, preferred_element_type=jnp.float32) / total
        return (weighted.astype(jnp.bfloat16), row_max[:, 0] + jnp.log(total[:, 0]))
    outputs, log_totals = lax.map(one_head, head_ids)
    log_totals = jnp.where(query_live[None, :], log_totals, 0.0)
    return (jnp.transpose(outputs, (1, 0, 2)), log_totals)

def reference(queries, key_row_matrix, value_row_matrix, residual, out_weight, doc_bounds, owner_plan):
    query_seq = queries.reshape(PACKED_TOKENS, QUERY_HEADS, HEAD_SIZE)
    key_sequence = key_row_matrix.reshape(PACKED_TOKENS, KEY_VALUE_HEADS, HEAD_SIZE)
    value_sequence = value_row_matrix.reshape(PACKED_TOKENS, KEY_VALUE_HEADS, HEAD_SIZE)

    def one_owner(attended, owner):
        first_block, end_block = owner_span(doc_bounds, owner_plan, owner, PACKED_TOKENS, BLOCK_POSITIONS)
        positions, is_live = slot_positions(first_block, end_block, N_CP, BLOCK_POSITIONS)
        safe_rows = jnp.where(is_live, positions, 0).astype(jnp.int32)
        slot_docs = doc_lookup(doc_bounds, positions)
        outputs, log_totals = attend_block(query_seq[safe_rows], key_sequence[safe_rows], value_sequence[safe_rows], positions, slot_docs, is_live, positions, slot_docs, is_live, GROUP)
        target_rows = jnp.where(is_live, positions, PACKED_TOKENS).astype(jnp.int32)
        attended = attended.at[target_rows].set(outputs, mode='drop')
        return (attended, log_totals)
    attended, stats = lax.scan(one_owner, jnp.zeros((PACKED_TOKENS, QUERY_HEADS, HEAD_SIZE), jnp.bfloat16), jnp.arange(N_CP, dtype=jnp.int32))
    projected = jnp.dot(attended.reshape(PACKED_TOKENS, QUERY_HEADS * HEAD_SIZE), out_weight.reshape(QUERY_HEADS * HEAD_SIZE, DWIN), preferred_element_type=jnp.float32)
    mixed = (residual.reshape(PACKED_TOKENS, DWIN).astype(jnp.float32) + projected).astype(jnp.bfloat16)
    return (mixed.reshape(DEVICE_BLOCKS, OWNER_ROW_SLOTS, DWIN), stats)
```

```python
import math

import jax
import jax.numpy as jnp
from jax import lax
from jax.experimental import pallas as pl
from jax.experimental.pallas import tpu as pltpu
from jax.sharding import Mesh, PartitionSpec as P

HEAD_SIZE = 128
MASKED = -1e30
SCALE = 1.0 / math.sqrt(HEAD_SIZE)
LOG2E = math.log2(math.e)

AXES = ("zh", "zl", "x", "y", "c")
SIZES = (4, 4, 4, 4, 2)
CP = ("zh", "zl", "x")
TP = ("y", "c")
NEAR = ("zl", "x")

HEADS = 8
ROWS = 128


def attend_kernel(where_ref, bounds_ref, query_ref, far_ref, near_ref, out_ref, total_ref):
    zh, beta = where_ref[0], where_ref[1]
    row_iota = lax.broadcasted_iota(jnp.int32, (ROWS, ROWS), 0)
    lane_iota = lax.broadcasted_iota(jnp.int32, (ROWS, ROWS), 1)
    bounds = bounds_ref[...]
    for r in range(2):
        b = 2 * beta + r
        query_pos = 512 * b + 128 * zh + row_iota
        start = jnp.max(
            jnp.where(bounds <= query_pos, bounds, 0).astype(jnp.float32), axis=1, keepdims=True
        ).astype(jnp.int32)
        biases = []
        for zk in range(4):
            key_pos = 512 * (b - (zk >= zh).astype(jnp.int32)) + 128 * zk + lane_iota
            biases.append(jnp.where(key_pos >= start, 0.0, MASKED))
        key_pos = 512 * b + 128 * zh + lane_iota
        biases.append(jnp.where((key_pos >= start) & (key_pos <= query_pos), 0.0, MASKED))
        bias = jnp.concatenate(biases, axis=1)
        keys = jnp.concatenate([far_ref[zk, r, :, :HEAD_SIZE] for zk in range(4)] + [near_ref[r, :, :HEAD_SIZE]], axis=0)
        values = jnp.concatenate([far_ref[zk, r, :, HEAD_SIZE:] for zk in range(4)] + [near_ref[r, :, HEAD_SIZE:]], axis=0)
        columns = []
        for h in range(HEADS):
            lanes = slice(h * HEAD_SIZE, (h + 1) * HEAD_SIZE)
            scores = lax.dot_general(
                query_ref[r, :, lanes], keys, (((1,), (1,)), ((), ())),
                preferred_element_type=jnp.float32,
            ) + bias
            row_max = jnp.max(scores, axis=1, keepdims=True)
            expo = jnp.exp2((scores - row_max) * (SCALE * LOG2E))
            total = jnp.sum(expo, axis=1, keepdims=True)
            weighted = jnp.dot(expo.astype(jnp.bfloat16), values, preferred_element_type=jnp.float32)
            out_ref[r, :, lanes] = (weighted / total).astype(jnp.bfloat16)
            columns.append(row_max * SCALE + jnp.log(total))
        total_ref[r] = jnp.concatenate(columns, axis=1).T


def attend(where, bounds, query, far, near):
    vmem = pl.BlockSpec(memory_space=pltpu.VMEM)
    return pl.pallas_call(
        attend_kernel,
        out_shape=(
            jax.ShapeDtypeStruct((2, ROWS, HEADS * HEAD_SIZE), jnp.bfloat16),
            jax.ShapeDtypeStruct((2, HEADS, ROWS), jnp.float32),
        ),
        in_specs=[pl.BlockSpec(memory_space=pltpu.SMEM), vmem, vmem, vmem, vmem],
        out_specs=(vmem, vmem),
        compiler_params=pltpu.CompilerParams(vmem_limit_bytes=32 * 1024 * 1024),
        cost_estimate=pl.CostEstimate(
            flops=2 * 2 * 2 * 1024 * 640 * 128, bytes_accessed=2 * 1024 * 1024, transcendentals=2 * 1024 * 640
        ),
    )(where, bounds, query, far, near)


def swap(source, axes, split=0, concat=0):
    return lax.all_to_all(source, axes, split_axis=split, concat_axis=concat, tiled=True)


def local(queries, key_rows, value_rows, residual, out_weight, doc_bounds, owner_plan):
    bf16, f32, i32 = jnp.bfloat16, jnp.float32, jnp.int32
    zh, zl, x = (lax.axis_index(a).astype(i32) for a in CP)
    core = lax.axis_index("c")
    beta = 4 * zl + x

    weight = out_weight.reshape(8, 2, 4, 2, 4, 128).transpose(4, 1, 0, 3, 2, 5).reshape(8, 8, 1024)
    weight = swap(weight, "x")

    both = jnp.concatenate([key_rows, value_rows], axis=2)
    pairs = both.reshape(16, 2, 8, 256)
    before = jnp.concatenate([pairs[:1, 1:], pairs[:-1, 1:]], axis=0)
    near3 = swap(jnp.concatenate([before, pairs], axis=1), NEAR)
    near3 = near3.transpose(1, 0, 2, 3).reshape(3, ROWS, 256)
    targets = jnp.arange(4, dtype=i32)[:, None, None, None]
    far = swap(jnp.where(targets <= zh, near3[None, :2], near3[None, 1:]), "zh")

    query = swap(queries, NEAR, 0, 1)

    gathered = lax.all_gather(weight, ("zh", "zl"), axis=0, tiled=True)
    gathered = gathered.transpose(1, 0, 2).reshape(1024, 1024)

    attended, totals = attend(
        jnp.stack([zh, beta]), doc_bounds[:128].reshape(1, 128), query, far, near3[1:]
    )

    blocks = 64 * (2 * beta + jnp.arange(2, dtype=i32))[:, None] + 16 * zh + jnp.arange(16, dtype=i32)[None, :]
    docs = jnp.sum((doc_bounds[None, None, 1:] <= 8 * blocks[:, :, None]).astype(i32), axis=2)
    doc_ids = jnp.arange(128, dtype=i32)
    owners = jnp.sum(jnp.where(docs[:, :, None] == doc_ids, owner_plan, 0), axis=2)
    owners = jnp.repeat(owners, 8, axis=1)
    owner_ids = jnp.arange(64, dtype=i32)[:, None]
    packed = sum(
        jnp.where((owners[r][None, :] == owner_ids)[:, None, :], totals[r][None], 0.0) for r in range(2)
    )
    slots = swap(packed, CP).reshape(4, 16, 8, 128)
    stats = jnp.sum(slots, axis=1).transpose(1, 0, 2).reshape(1, 8, 512)

    attended = attended.reshape(1, 256, 1024)
    wide = swap(jnp.broadcast_to(attended, (4, 256, 1024)), "x").reshape(1024, 1024)
    halves = gathered.reshape(1024, 2, 512)
    theirs = jnp.dot(
        wide, lax.dynamic_index_in_dim(halves, 1 - core, 1, keepdims=False), preferred_element_type=f32
    ).astype(bf16)
    ours = jnp.dot(wide, lax.dynamic_index_in_dim(halves, core, 1, keepdims=False), preferred_element_type=f32)
    got = lax.ppermute(theirs, "c", [(0, 1), (1, 0)])
    pair = (ours + got.astype(f32)).astype(bf16)
    parts = swap(pair.reshape(1024, 4, 128).transpose(1, 0, 2), "y")
    summed = jnp.sum(parts.astype(f32), axis=0).astype(bf16)
    summed = summed.reshape(8, 16, 8, 128).transpose(1, 0, 2, 3)
    home = swap(summed, NEAR).reshape(4, 4, 8, 8, 128)
    home = home.transpose(0, 2, 3, 1, 4).reshape(32, 8, 512)
    mixed = (residual.astype(f32) + home.astype(f32)).astype(bf16)
    return mixed, stats


def solution(mesh):
    fine = Mesh(mesh.devices.reshape(SIZES), AXES)
    rows = P(None, CP, TP)
    return jax.shard_map(
        local,
        mesh=fine,
        in_specs=(rows, rows, rows, rows, P(TP, CP, None), P(), P()),
        out_specs=(rows, P(CP, TP, None)),
        check_vma=False,
    )
```

```python
import math

import jax
import jax.numpy as jnp
from jax import lax
from jax.experimental import pallas as pl
from jax.experimental.pallas import tpu as pltpu
from jax.sharding import Mesh, PartitionSpec as P

HEAD_SIZE = 128
MASKED = -1e30
SCALE = 1.0 / math.sqrt(HEAD_SIZE)
LOG2E = math.log2(math.e)

AXES = ("za", "zb", "zl", "x", "y", "c")
SIZES = (2, 2, 4, 4, 4, 2)
CP = ("za", "zb", "zl", "x")
ZH = ("za", "zb")
Z = ("za", "zb", "zl")
TP = ("y", "c")
NEAR = ("zl", "x")

HEADS = 8
ROWS = 128


def attend_kernel(where_ref, bounds_ref, query_ref, far_ref, near_ref, out_ref, total_ref):
    zh, beta = where_ref[0], where_ref[1]
    row_iota = lax.broadcasted_iota(jnp.int32, (ROWS, ROWS), 0)
    lane_iota = lax.broadcasted_iota(jnp.int32, (ROWS, ROWS), 1)
    bounds = bounds_ref[...]
    for r in range(2):
        b = 2 * beta + r
        query_pos = 512 * b + 128 * zh + row_iota
        start = jnp.max(
            jnp.where(bounds <= query_pos, bounds, 0).astype(jnp.float32), axis=1, keepdims=True
        ).astype(jnp.int32)
        biases = []
        for step in range(4):
            zk = lax.rem(zh - step + 4, 4)
            key_pos = 512 * (b - (zk >= zh).astype(jnp.int32)) + 128 * zk + lane_iota
            biases.append(jnp.where(key_pos >= start, 0.0, MASKED))
        key_pos = 512 * b + 128 * zh + lane_iota
        biases.append(jnp.where((key_pos >= start) & (key_pos <= query_pos), 0.0, MASKED))
        bias = jnp.concatenate(biases, axis=1)
        keys = jnp.concatenate([far_ref[zk, r, :, :HEAD_SIZE] for zk in range(4)] + [near_ref[r, :, :HEAD_SIZE]], axis=0)
        values = jnp.concatenate([far_ref[zk, r, :, HEAD_SIZE:] for zk in range(4)] + [near_ref[r, :, HEAD_SIZE:]], axis=0)
        columns = []
        for h in range(HEADS):
            lanes = slice(h * HEAD_SIZE, (h + 1) * HEAD_SIZE)
            scores = lax.dot_general(
                query_ref[r, :, lanes], keys, (((1,), (1,)), ((), ())),
                preferred_element_type=jnp.float32,
            ) + bias
            row_max = jnp.max(scores, axis=1, keepdims=True)
            expo = jnp.exp2((scores - row_max) * (SCALE * LOG2E))
            total = jnp.sum(expo, axis=1, keepdims=True)
            weighted = jnp.dot(expo.astype(jnp.bfloat16), values, preferred_element_type=jnp.float32)
            rows = (weighted / total).astype(jnp.bfloat16)
            for copy in range(4):
                out_ref[copy, r, :, lanes] = rows
            columns.append(row_max * SCALE + jnp.log(total))
        total_ref[r] = jnp.concatenate(columns, axis=1).T


def attend(where, bounds, query, far, near):
    vmem = pl.BlockSpec(memory_space=pltpu.VMEM)
    return pl.pallas_call(
        attend_kernel,
        out_shape=(
            jax.ShapeDtypeStruct((4, 2, ROWS, HEADS * HEAD_SIZE), jnp.bfloat16),
            jax.ShapeDtypeStruct((2, HEADS, ROWS), jnp.float32),
        ),
        in_specs=[pl.BlockSpec(memory_space=pltpu.SMEM), vmem, vmem, vmem, vmem],
        out_specs=(vmem, vmem),
        compiler_params=pltpu.CompilerParams(vmem_limit_bytes=32 * 1024 * 1024),
        cost_estimate=pl.CostEstimate(
            flops=2 * 2 * 2 * 1024 * 640 * 128, bytes_accessed=2 * 1024 * 1024, transcendentals=2 * 1024 * 640
        ),
    )(where, bounds, query, far, near)


def project_kernel(rows_ref, weight_ref, out_ref):
    for part in range(4):
        rows = slice(part * 256, (part + 1) * 256)
        product = jnp.dot(rows_ref[rows], weight_ref[...], preferred_element_type=jnp.float32)
        for y in range(4):
            out_ref[y, rows] = product[:, y * 128 : (y + 1) * 128].astype(out_ref.dtype)


def project(rows, weight, half, dtype):
    vmem = pl.BlockSpec(memory_space=pltpu.VMEM)
    return pl.pallas_call(
        project_kernel,
        grid=(1,),
        out_shape=jax.ShapeDtypeStruct((4, 1024, 128), dtype),
        in_specs=[vmem, pl.BlockSpec((1024, 512), lambda i: (0, half))],
        out_specs=vmem,
        compiler_params=pltpu.CompilerParams(vmem_limit_bytes=32 * 1024 * 1024),
        cost_estimate=pl.CostEstimate(
            flops=2 * 1024 * 1024 * 512, bytes_accessed=4 * 1024 * 1024, transcendentals=0
        ),
    )(rows, weight)


def swap(source, axes, split=0, concat=0):
    return lax.all_to_all(source, axes, split_axis=split, concat_axis=concat, tiled=True)


def shift(source, axes, size, step):
    return lax.ppermute(source, axes, [(i, (i + step) % size) for i in range(size)])


def local(queries, key_rows, value_rows, residual, out_weight, doc_bounds, owner_plan):
    bf16, f32, i32 = jnp.bfloat16, jnp.float32, jnp.int32
    zh, zl, x = lax.axis_index(ZH), lax.axis_index("zl"), lax.axis_index("x")
    core = lax.axis_index("c")
    beta = 4 * zl + x

    weight = out_weight.reshape(8, 2, 4, 2, 4, 128)
    weight = jnp.where(core == 0, weight, jnp.flip(weight, 3)).transpose(4, 0, 1, 3, 2, 5).reshape(4, 8, 2, 1024)
    weight = swap(weight, "x").transpose(1, 0, 2, 3).reshape(8, 8, 1024)
    gathered = lax.all_gather(weight, Z, axis=0, tiled=False)
    gathered = gathered.transpose(1, 0, 2, 3).reshape(1024, 1024)

    both = jnp.concatenate([key_rows, value_rows], axis=2)
    pairs = both.reshape(16, 2, 8, 256)
    before = jnp.concatenate([pairs[:1, 1:], pairs[:-1, 1:]], axis=0)
    near3, weight = lax.optimization_barrier((jnp.concatenate([before, pairs], axis=1), weight))
    near3 = swap(near3, NEAR)
    near3 = near3.transpose(1, 0, 2, 3).reshape(3, ROWS, 256)

    far = [near3[:2]]
    for step in (1, 2, 3):
        rows = jnp.where(zh + step >= 4, near3[:2], near3[1:])
        far.append(shift(rows, ZH, 4, step))
    far = jnp.stack(far)

    queries, near3 = lax.optimization_barrier((queries, near3))
    query = swap(queries, NEAR, 0, 1)

    attended, totals = attend(
        jnp.stack([zh, beta]), doc_bounds[:128].reshape(1, 128), query, far, near3[1:]
    )

    totals = totals.astype(bf16)
    lanes = [totals] + [shift(totals, ZH, 4, step) for step in (1, 2, 3)]
    groups = [(zh - step) % 4 for step in range(4)]
    blocks = 64 * (2 * beta + jnp.arange(2, dtype=i32))[:, None, None] + jnp.arange(16, dtype=i32)
    blocks = blocks + 16 * jnp.stack(groups)[None, :, None]
    docs = jnp.sum((doc_bounds[1:] <= 8 * blocks[..., None]).astype(i32), axis=-1)
    owners = jnp.sum(jnp.where(docs[..., None] == jnp.arange(128, dtype=i32), owner_plan, 0), axis=-1)
    owners = jnp.repeat(owners, 8, axis=2) - 16 * zh
    receivers = jnp.arange(16, dtype=i32)[:, None, None, None]
    lanes = jnp.stack(lanes)
    packed = jnp.zeros((), bf16)
    for r in range(2):
        packed = packed + jnp.where(owners[r][None, :, None, :] == receivers, lanes[None, :, r], jnp.zeros((), bf16))

    wide = swap(attended.reshape(4, 256, 1024), "x").reshape(1024, 1024)
    wide, packed = lax.optimization_barrier((wide, packed))
    theirs = project(wide, gathered, 1, bf16)
    got = lax.ppermute(theirs, "c", [(0, 1), (1, 0)])
    ours = project(wide, gathered, 0, f32)
    ours, got = lax.optimization_barrier((ours, got))
    parts = swap((ours + got.astype(f32)).astype(bf16), "y")
    summed = jnp.sum(parts.astype(f32), axis=0).astype(bf16)
    summed = summed.reshape(8, 16, 8, 128).transpose(1, 0, 2, 3)
    home = swap(jnp.concatenate([summed, packed], axis=1), NEAR)
    stats = jnp.sum(home[:, 8:].astype(f32), axis=0)
    stats = jnp.concatenate([lax.dynamic_index_in_dim(stats, (zh - k) % 4, 0, keepdims=False) for k in range(4)], axis=1)
    stats = stats.reshape(1, 8, 512)
    home = home[:, :8].reshape(4, 4, 8, 8, 128).transpose(0, 2, 3, 1, 4).reshape(32, 8, 512)
    mixed = (residual.astype(f32) + home.astype(f32)).astype(bf16)
    return mixed, stats


def solution(mesh):
    fine = Mesh(mesh.devices.reshape(SIZES), AXES)
    rows = P(None, CP, TP)
    return jax.shard_map(
        local,
        mesh=fine,
        in_specs=(rows, rows, rows, rows, P(TP, CP, None), P(), P()),
        out_specs=(rows, P(CP, TP, None)),
        check_vma=False,
    )
```

```python
import math

import jax
import jax.numpy as jnp
from jax import lax
from jax.experimental import pallas as pl
from jax.experimental.pallas import tpu as pltpu
from jax.sharding import Mesh, PartitionSpec as P

HEAD_SIZE = 128
MASKED = -1e30
SCALE = 1.0 / math.sqrt(HEAD_SIZE)
LOG2E = math.log2(math.e)

AXES = ("za", "zb", "zl", "x", "y", "c")
SIZES = (2, 2, 4, 4, 4, 2)
CP = ("za", "zb", "zl", "x")
ZH = ("za", "zb")
Z = ("za", "zb", "zl")
TP = ("y", "c")
NEAR = ("zl", "x")

HEADS = 8
ROWS = 128


def attend_kernel(where_ref, bounds_ref, query_ref, far_ref, near_ref, out_ref, total_ref):
    zh, beta = where_ref[0], where_ref[1]
    row_iota = lax.broadcasted_iota(jnp.int32, (ROWS, ROWS), 0)
    lane_iota = lax.broadcasted_iota(jnp.int32, (ROWS, ROWS), 1)
    bounds = bounds_ref[...]
    for r in range(2):
        b = 2 * beta + r
        query_pos = 512 * b + 128 * zh + row_iota
        start = jnp.max(
            jnp.where(bounds <= query_pos, bounds, 0).astype(jnp.float32), axis=1, keepdims=True
        ).astype(jnp.int32)
        biases = []
        for step in range(4):
            zk = lax.rem(zh - step + 4, 4)
            key_pos = 512 * (b - (zk >= zh).astype(jnp.int32)) + 128 * zk + lane_iota
            biases.append(jnp.where(key_pos >= start, 0.0, MASKED))
        key_pos = 512 * b + 128 * zh + lane_iota
        biases.append(jnp.where((key_pos >= start) & (key_pos <= query_pos), 0.0, MASKED))
        bias = jnp.concatenate(biases, axis=1)
        keys = jnp.concatenate([far_ref[zk, r, :, :HEAD_SIZE] for zk in range(4)] + [near_ref[r, :, :HEAD_SIZE]], axis=0)
        values = jnp.concatenate([far_ref[zk, r, :, HEAD_SIZE:] for zk in range(4)] + [near_ref[r, :, HEAD_SIZE:]], axis=0)
        columns = []
        for h in range(HEADS):
            lanes = slice(h * HEAD_SIZE, (h + 1) * HEAD_SIZE)
            scores = lax.dot_general(
                query_ref[r, :, lanes], keys, (((1,), (1,)), ((), ())),
                preferred_element_type=jnp.float32,
            ) + bias
            row_max = jnp.max(scores, axis=1, keepdims=True)
            expo = jnp.exp2((scores - row_max) * (SCALE * LOG2E))
            total = jnp.sum(expo, axis=1, keepdims=True)
            weighted = jnp.dot(expo.astype(jnp.bfloat16), values, preferred_element_type=jnp.float32)
            rows = (weighted / total).astype(jnp.bfloat16)
            for copy in range(4):
                out_ref[copy, r, :, lanes] = rows
            columns.append(row_max * SCALE + jnp.log(total))
        total_ref[r] = jnp.concatenate(columns, axis=1).T


def attend(where, bounds, query, far, near):
    vmem = pl.BlockSpec(memory_space=pltpu.VMEM)
    return pl.pallas_call(
        attend_kernel,
        out_shape=(
            jax.ShapeDtypeStruct((4, 2, ROWS, HEADS * HEAD_SIZE), jnp.bfloat16),
            jax.ShapeDtypeStruct((2, HEADS, ROWS), jnp.float32),
        ),
        in_specs=[pl.BlockSpec(memory_space=pltpu.SMEM), vmem, vmem, vmem, vmem],
        out_specs=(vmem, vmem),
        compiler_params=pltpu.CompilerParams(vmem_limit_bytes=32 * 1024 * 1024),
        cost_estimate=pl.CostEstimate(
            flops=2 * 2 * 2 * 1024 * 640 * 128, bytes_accessed=2 * 1024 * 1024, transcendentals=2 * 1024 * 640
        ),
    )(where, bounds, query, far, near)


def project_kernel(core_ref, own_ref, other_ref, own_weight_ref, other_weight_ref, out_ref):
    del core_ref
    product = jnp.dot(own_ref[...], own_weight_ref[...], preferred_element_type=jnp.float32)
    product += jnp.dot(other_ref[...], other_weight_ref[...], preferred_element_type=jnp.float32)
    for y in range(4):
        out_ref[y] = product[:, y * 128 : (y + 1) * 128].astype(out_ref.dtype)


def project(core, own, other, weight):
    rows = pl.BlockSpec((512, 1024), lambda i, core: (i, 0))
    return pl.pallas_call(
        project_kernel,
        grid_spec=pltpu.PrefetchScalarGridSpec(
            num_scalar_prefetch=1,
            grid=(2,),
            in_specs=[
                rows,
                rows,
                pl.BlockSpec((1024, 512), lambda i, core: (core[0], 0)),
                pl.BlockSpec((1024, 512), lambda i, core: (1 - core[0], 0)),
            ],
            out_specs=pl.BlockSpec((4, 512, 128), lambda i, core: (0, i, 0)),
        ),
        out_shape=jax.ShapeDtypeStruct((4, 1024, 128), jnp.bfloat16),
        compiler_params=pltpu.CompilerParams(vmem_limit_bytes=32 * 1024 * 1024),
        cost_estimate=pl.CostEstimate(
            flops=2 * 1024 * 2048 * 512, bytes_accessed=7 * 1024 * 1024, transcendentals=0
        ),
    )(core.reshape(1), own, other, weight, weight)


def arrange_kernel(source_ref, out_ref):
    for k in range(out_ref.shape[0]):
        out_ref[k] = source_ref[:, k]


def arrange(source):
    return pl.pallas_call(
        arrange_kernel,
        grid=(4,),
        out_shape=jax.ShapeDtypeStruct(source.shape, source.dtype),
        in_specs=[pl.BlockSpec((16, 4, 8, 512), lambda i: (0, i, 0, 0))],
        out_specs=pl.BlockSpec((4, 16, 8, 512), lambda i: (i, 0, 0, 0)),
        compiler_params=pltpu.CompilerParams(vmem_limit_bytes=32 * 1024 * 1024),
        cost_estimate=pl.CostEstimate(flops=10**11, bytes_accessed=4 * 1024 * 1024, transcendentals=0),
    )(source)


def swap(source, axes, split=0, concat=0):
    return lax.all_to_all(source, axes, split_axis=split, concat_axis=concat, tiled=True)


def shift(source, axes, size, step):
    return lax.ppermute(source, axes, [(i, (i + step) % size) for i in range(size)])


def local(queries, key_rows, value_rows, residual, out_weight, doc_bounds, owner_plan):
    bf16, f32, i32 = jnp.bfloat16, jnp.float32, jnp.int32
    zh, zl, x = lax.axis_index(ZH), lax.axis_index("zl"), lax.axis_index("x")
    core = lax.axis_index("c")
    beta = 4 * zl + x

    weight = out_weight.reshape(8, 2, 4, 2, 4, 128).transpose(4, 3, 0, 1, 2, 5).reshape(8, 16, 512)
    weight = swap(weight, ("x", "c")).reshape(4, 2, 8, 2, 512)
    weight = weight.transpose(1, 2, 0, 3, 4).reshape(16, 8, 512)
    weight, key_rows, value_rows = lax.optimization_barrier((weight, key_rows, value_rows))
    gathered = lax.all_gather(weight, Z, axis=0, tiled=False)
    gathered = arrange(gathered).reshape(2048, 512)

    both = jnp.concatenate([key_rows, value_rows], axis=2)
    pairs = both.reshape(16, 2, 8, 256)
    before = jnp.concatenate([pairs[:1, 1:], pairs[:-1, 1:]], axis=0)
    near3 = swap(jnp.concatenate([before, pairs], axis=1), NEAR)
    near3 = near3.transpose(1, 0, 2, 3).reshape(3, ROWS, 256)

    far = [near3[:2]]
    for step in (1, 2, 3):
        rows = jnp.where(zh + step >= 4, near3[:2], near3[1:])
        far.append(shift(rows, ZH, 4, step))
    far = jnp.stack(far)

    queries, near3 = lax.optimization_barrier((queries, near3))
    query = swap(queries, NEAR, 0, 1)

    attended, totals = attend(
        jnp.stack([zh, beta]), doc_bounds[:128].reshape(1, 128), query, far, near3[1:]
    )

    totals = totals.astype(bf16)
    lanes = [totals] + [shift(totals, ZH, 4, step) for step in (1, 2, 3)]
    groups = [(zh - step) % 4 for step in range(4)]
    blocks = 64 * (2 * beta + jnp.arange(2, dtype=i32))[:, None, None] + jnp.arange(16, dtype=i32)
    blocks = blocks + 16 * jnp.stack(groups)[None, :, None]
    docs = jnp.sum((doc_bounds[1:] <= 8 * blocks[..., None]).astype(i32), axis=-1)
    owners = jnp.sum(jnp.where(docs[..., None] == jnp.arange(128, dtype=i32), owner_plan, 0), axis=-1)
    owners = jnp.repeat(owners, 8, axis=2) - 16 * zh
    receivers = jnp.arange(16, dtype=i32)[:, None, None, None]
    lanes = jnp.stack(lanes)
    packed = jnp.zeros((), bf16)
    for r in range(2):
        packed = packed + jnp.where(owners[r][None, :, None, :] == receivers, lanes[None, :, r], jnp.zeros((), bf16))

    wide = swap(attended.reshape(4, 256, 1024), "x").reshape(1024, 1024)
    wide, packed = lax.optimization_barrier((wide, packed))
    other = shift(wide, "c", 2, 1)
    parts = swap(project(core.astype(i32), wide, other, gathered), "y")
    summed = jnp.sum(parts.astype(f32), axis=0).astype(bf16)
    summed = summed.reshape(8, 16, 8, 128).transpose(1, 0, 2, 3)
    home = swap(jnp.concatenate([summed, packed], axis=1), NEAR)
    stats = jnp.sum(home[:, 8:].astype(f32), axis=0)
    stats = jnp.concatenate([lax.dynamic_index_in_dim(stats, (zh - k) % 4, 0, keepdims=False) for k in range(4)], axis=1)
    stats = stats.reshape(1, 8, 512)
    home = home[:, :8].reshape(4, 4, 8, 8, 128).transpose(0, 2, 3, 1, 4).reshape(32, 8, 512)
    mixed = (residual.astype(f32) + home.astype(f32)).astype(bf16)
    return mixed, stats


def solution(mesh):
    fine = Mesh(mesh.devices.reshape(SIZES), AXES)
    rows = P(None, CP, TP)
    return jax.shard_map(
        local,
        mesh=fine,
        in_specs=(rows, rows, rows, rows, P(TP, CP, None), P(), P()),
        out_specs=(rows, P(CP, TP, None)),
        check_vma=False,
    )
```

```python
import math

import jax
import jax.numpy as jnp
from jax import lax
from jax.experimental import pallas as pl
from jax.experimental.pallas import tpu as pltpu
from jax.sharding import Mesh, PartitionSpec as P

HEAD_SIZE = 128
MASKED = -1e30
SCALE = 1.0 / math.sqrt(HEAD_SIZE)
LOG2E = math.log2(math.e)

AXES = ("za", "zb", "zl", "x", "y", "c")
SIZES = (2, 2, 4, 4, 4, 2)
CP = ("za", "zb", "zl", "x")
ZH = ("za", "zb")
Z = ("za", "zb", "zl")
TP = ("y", "c")
NEAR = ("zl", "x")

HEADS = 8
ROWS = 128


def attend_kernel(where_ref, bounds_ref, query_ref, far_ref, near_ref, out_ref, total_ref):
    zh, beta = where_ref[0], where_ref[1]
    row_iota = lax.broadcasted_iota(jnp.int32, (ROWS, ROWS), 0)
    lane_iota = lax.broadcasted_iota(jnp.int32, (ROWS, ROWS), 1)
    bounds = bounds_ref[...]
    for r in range(2):
        b = 2 * beta + r
        query_pos = 512 * b + 128 * zh + row_iota
        start = jnp.max(
            jnp.where(bounds <= query_pos, bounds, 0).astype(jnp.float32), axis=1, keepdims=True
        ).astype(jnp.int32)
        biases = []
        for step in range(4):
            zk = lax.rem(zh - step + 4, 4)
            key_pos = 512 * (b - (zk >= zh).astype(jnp.int32)) + 128 * zk + lane_iota
            biases.append(jnp.where(key_pos >= start, 0.0, MASKED))
        key_pos = 512 * b + 128 * zh + lane_iota
        biases.append(jnp.where((key_pos >= start) & (key_pos <= query_pos), 0.0, MASKED))
        bias = jnp.concatenate(biases, axis=1)
        keys = jnp.concatenate([far_ref[zk, r, :, :HEAD_SIZE] for zk in range(4)] + [near_ref[r, :, :HEAD_SIZE]], axis=0)
        values = jnp.concatenate([far_ref[zk, r, :, HEAD_SIZE:] for zk in range(4)] + [near_ref[r, :, HEAD_SIZE:]], axis=0)
        columns = []
        for h in range(HEADS):
            lanes = slice(h * HEAD_SIZE, (h + 1) * HEAD_SIZE)
            scores = lax.dot_general(
                query_ref[r, :, lanes], keys, (((1,), (1,)), ((), ())),
                preferred_element_type=jnp.float32,
            ) + bias
            row_max = jnp.max(scores, axis=1, keepdims=True)
            expo = jnp.exp2((scores - row_max) * (SCALE * LOG2E))
            total = jnp.sum(expo, axis=1, keepdims=True)
            weighted = jnp.dot(expo.astype(jnp.bfloat16), values, preferred_element_type=jnp.float32)
            rows = (weighted / total).astype(jnp.bfloat16)
            for copy in range(4):
                out_ref[copy, r, :, lanes] = rows
            columns.append(row_max * SCALE + jnp.log(total))
        total_ref[r] = jnp.concatenate(columns, axis=1).T


def attend(where, bounds, query, far, near):
    vmem = pl.BlockSpec(memory_space=pltpu.VMEM)
    return pl.pallas_call(
        attend_kernel,
        out_shape=(
            jax.ShapeDtypeStruct((4, 2, ROWS, HEADS * HEAD_SIZE), jnp.bfloat16),
            jax.ShapeDtypeStruct((2, HEADS, ROWS), jnp.float32),
        ),
        in_specs=[pl.BlockSpec(memory_space=pltpu.SMEM), vmem, vmem, vmem, vmem],
        out_specs=(vmem, vmem),
        compiler_params=pltpu.CompilerParams(vmem_limit_bytes=32 * 1024 * 1024),
        cost_estimate=pl.CostEstimate(
            flops=2 * 2 * 2 * 1024 * 640 * 128, bytes_accessed=2 * 1024 * 1024, transcendentals=2 * 1024 * 640
        ),
    )(where, bounds, query, far, near)


def project_kernel(core_ref, rows_ref, weight_ref, out_ref):
    del core_ref
    for part in range(4):
        rows = slice(part * 256, (part + 1) * 256)
        product = jnp.dot(rows_ref[rows], weight_ref[...], preferred_element_type=jnp.float32)
        for y in range(4):
            out_ref[y, rows] = product[:, y * 128 : (y + 1) * 128].astype(out_ref.dtype)


def project(core, rows, weight, dtype):
    return pl.pallas_call(
        project_kernel,
        grid_spec=pltpu.PrefetchScalarGridSpec(
            num_scalar_prefetch=1,
            grid=(1,),
            in_specs=[
                pl.BlockSpec(memory_space=pltpu.VMEM),
                pl.BlockSpec((1024, 512), lambda i, core: (0, core[0])),
            ],
            out_specs=pl.BlockSpec(memory_space=pltpu.VMEM),
        ),
        out_shape=jax.ShapeDtypeStruct((4, 1024, 128), dtype),
        compiler_params=pltpu.CompilerParams(vmem_limit_bytes=32 * 1024 * 1024),
        cost_estimate=pl.CostEstimate(
            flops=2 * 1024 * 1024 * 512, bytes_accessed=4 * 1024 * 1024, transcendentals=0
        ),
    )(core.astype(jnp.int32).reshape(1), rows, weight)


def swap(source, axes, split=0, concat=0):
    return lax.all_to_all(source, axes, split_axis=split, concat_axis=concat, tiled=True)


def shift(source, axes, size, step):
    return lax.ppermute(source, axes, [(i, (i + step) % size) for i in range(size)])


def local(queries, key_rows, value_rows, residual, out_weight, doc_bounds, owner_plan):
    bf16, f32, i32 = jnp.bfloat16, jnp.float32, jnp.int32
    zh, zl, x = lax.axis_index(ZH), lax.axis_index("zl"), lax.axis_index("x")
    core = lax.axis_index("c")
    beta = 4 * zl + x

    weight = out_weight.reshape(8, 2, 4, 2, 4, 128)
    weight = weight.transpose(4, 0, 1, 3, 2, 5).reshape(4, 8, 2, 1024)
    weight = swap(weight, "x").transpose(1, 0, 2, 3).reshape(8, 8, 1024)
    gathered = lax.all_gather(weight, Z, axis=0, tiled=False)
    gathered = gathered.transpose(1, 0, 2, 3).reshape(1024, 1024)

    both = jnp.concatenate([key_rows, value_rows], axis=2)
    pairs = both.reshape(16, 2, 8, 256)
    before = jnp.concatenate([pairs[:1, 1:], pairs[:-1, 1:]], axis=0)
    near3, weight = lax.optimization_barrier((jnp.concatenate([before, pairs], axis=1), weight))
    near3 = swap(near3, NEAR)
    near3 = near3.transpose(1, 0, 2, 3).reshape(3, ROWS, 256)

    far = [near3[:2]]
    for step in (1, 2, 3):
        rows = jnp.where(zh + step >= 4, near3[:2], near3[1:])
        far.append(shift(rows, ZH, 4, step))
    far = jnp.stack(far)

    queries, near3 = lax.optimization_barrier((queries, near3))
    query = swap(queries, NEAR, 0, 1)

    attended, totals = attend(
        jnp.stack([zh, beta]), doc_bounds[:128].reshape(1, 128), query, far, near3[1:]
    )

    totals = totals.astype(bf16)
    lanes = [totals] + [shift(totals, ZH, 4, step) for step in (1, 2, 3)]
    groups = [(zh - step) % 4 for step in range(4)]
    blocks = 64 * (2 * beta + jnp.arange(2, dtype=i32))[:, None, None] + jnp.arange(16, dtype=i32)
    blocks = blocks + 16 * jnp.stack(groups)[None, :, None]
    docs = jnp.sum((doc_bounds[1:] <= 8 * blocks[..., None]).astype(i32), axis=-1)
    owners = jnp.sum(jnp.where(docs[..., None] == jnp.arange(128, dtype=i32), owner_plan, 0), axis=-1)
    owners = jnp.repeat(owners, 8, axis=2) - 16 * zh
    receivers = jnp.arange(16, dtype=i32)[:, None, None, None]
    lanes = jnp.stack(lanes)
    packed = jnp.zeros((), bf16)
    for r in range(2):
        packed = packed + jnp.where(owners[r][None, :, None, :] == receivers, lanes[None, :, r], jnp.zeros((), bf16))

    wide = swap(attended.reshape(4, 256, 1024), "x").reshape(1024, 1024)
    wide, packed = lax.optimization_barrier((wide, packed))
    theirs = project(1 - core, wide, gathered, bf16)
    got = lax.ppermute(theirs, "c", [(0, 1), (1, 0)])
    ours = project(core, wide, gathered, f32)
    ours, got = lax.optimization_barrier((ours, got))
    parts = swap((ours + got.astype(f32)).astype(bf16), "y")
    summed = jnp.sum(parts.astype(f32), axis=0).astype(bf16)
    summed = summed.reshape(8, 16, 8, 128).transpose(1, 0, 2, 3)
    home = swap(jnp.concatenate([summed, packed], axis=1), NEAR)
    stats = jnp.sum(home[:, 8:].astype(f32), axis=0)
    stats = jnp.concatenate([lax.dynamic_index_in_dim(stats, (zh - k) % 4, 0, keepdims=False) for k in range(4)], axis=1)
    stats = stats.reshape(1, 8, 512)
    home = home[:, :8].reshape(4, 4, 8, 8, 128).transpose(0, 2, 3, 1, 4).reshape(32, 8, 512)
    mixed = (residual.astype(f32) + home.astype(f32)).astype(bf16)
    return mixed, stats


def solution(mesh):
    fine = Mesh(mesh.devices.reshape(SIZES), AXES)
    rows = P(None, CP, TP)
    return jax.shard_map(
        local,
        mesh=fine,
        in_specs=(rows, rows, rows, rows, P(TP, CP, None), P(), P()),
        out_specs=(rows, P(CP, TP, None)),
        check_vma=False,
    )
```
